32 devices in a mesh: dp: 4 (over y, x), seq: 8 (over z, core).
Axes of the slice: x: 2, y: 2, z: 4, core: 2. Of those that a mesh axis runs over, the one named last changes fastest.
Arguments:
- tokens: bfloat16 [4, 128, 128, 1024], P('dp', 'seq'), may hold values from -12 to 12
- lengths: int32 [4], P('dp'), may hold values from 8192 to 16384, as said below
- w_qkv: bfloat16 [3, 1024, 1024], replicated, may hold values from -0.1875 to 0.1875
- out_grad: bfloat16 [4, 128, 128, 1024], P('dp', 'seq'), may hold values from -6 to 6
Outputs:
- attention: bfloat16 [4, 128, 128, 1024], P('dp', 'seq')
- input_grad: bfloat16 [4, 128, 128, 1024], P('dp', 'seq')
- w_grads: float32 [3, 1024, 1024], P(None, 'seq', 'dp')
The draws below stay inside these ranges and needn't reach their ends.
Inputs may be any that keep to these rules, and one draw needn't show every extreme that they name: Samples at positions from lengths on are padding; some sequence is full and some has exactly 8192 valid samples.
All inputs are finite; a program needn't handle non-finite values.
Results may differ from the reference program's by a relative error of at most 0.04.
The reference program's roundings to bfloat16 on the way count: a program that leaves them out, or rounds other values in their place, can miss the bound.
Values may be sent and summed in bfloat16 or wider, within the bound.
No kernel may reach another device: no remote copies, remote signals or barrier semaphores. Data moves between devices by JAX's collectives and lax.ppermute only.
A program may use at most 192 MiB of HBM per device.

```python
import math
import jax
import jax.numpy as jnp
from jax import lax

D = 1024
HEADS = 8
HEAD_DIM = 128
ROWS = 128
STRIDE = 128
SAMPLES = 16384
SEQS = 4


def draw_tokens(key, part):
    shape = (SEQS, ROWS, STRIDE, D)
    base_key = jax.random.fold_in(jax.random.fold_in(key, 11), 0)
    values = jnp.clip(jax.random.normal(base_key, shape, jnp.float32), -6.0, 6.0)
    return values.astype(jnp.bfloat16)


def draw_lengths(key, part):
    first_key, second_key = jax.random.split(jax.random.fold_in(key, 23), 2)
    values = jax.random.randint(first_key, (SEQS,), SAMPLES // 2, SAMPLES + 1)
    order = jax.random.permutation(second_key, SEQS)
    values = values.at[order[0]].set(SAMPLES).at[order[1]].set(SAMPLES // 2)
    return values.astype(jnp.int32)


def shard_levels(stream_key, dims, cuts, smallest, high):
    factor_of = 1.0
    for axis_at, blocks in cuts:
        steps = jax.random.uniform(jax.random.fold_in(jax.random.fold_in(stream_key, 6), axis_at), (blocks,), jnp.float32, smallest / len(cuts), high / len(cuts))
        factor_of = factor_of * jnp.repeat(jnp.exp(steps), dims[axis_at] // blocks).reshape((-1,) + (1,) * (len(dims) - 1 - axis_at))
    return factor_of


def normal_values(own_key, dims, spread, reach, shards=(), kind=jnp.bfloat16):
    result = jax.random.normal(own_key, dims, jnp.float32) * spread
    if len(shards) > 0:
        result = shard_levels(own_key, dims, shards, -0.22, 0.18) * result
    return jnp.clip(result, min=-reach, max=reach).astype(kind)


def setup_inputs(seed: int = 0) -> dict:
    seeds = jax.random.split(jax.random.key(seed), 5)
    tokens = draw_tokens(jax.random.fold_in(seeds[4], 71), 0)
    lengths = draw_lengths(jax.random.fold_in(seeds[4], 71), 0)
    w_qkv = normal_values(seeds[2], (3, D, D), D ** -0.5, 0.1875)
    out_grad = normal_values(seeds[3], (SEQS, ROWS, STRIDE, D), 1.0, 6.0, ((0, 4), (1, 8)))
    return dict(tokens=tokens, lengths=lengths, w_qkv=w_qkv, out_grad=out_grad)


SCORE_FORM = 'bqhe,bkhe->bqhk'
APPLY_FORM = 'bqhk,bkhe->bqhe'
BACK_FORM = 'bqhk,bqhe->bkhe'

def rounded(values):
    return lax.optimization_barrier(values.astype(jnp.bfloat16)).astype(jnp.float32)

def swap_axes(values):
    return jnp.swapaxes(values, 0, 1)

def part_forward(query_h, key_h, value_h, allowed):
    scaling = 1.0 / math.sqrt(query_h.shape[-1])
    scores = jnp.where(allowed, jnp.einsum(SCORE_FORM, query_h, key_h) * scaling, -1e+30)
    highest = lax.optimization_barrier(jnp.max(scores, axis=-1))
    weights = jnp.where(allowed, jnp.exp(scores - highest[..., None]), 0.0)
    totals = lax.optimization_barrier(jnp.sum(weights, axis=-1))
    mixed = jnp.einsum(APPLY_FORM, rounded(weights), value_h)
    return (highest, totals, mixed)

def part_back(query_h, key_h, value_h, grad_h, allowed, log_total, delta):
    scaling = 1.0 / math.sqrt(query_h.shape[-1])
    scores = jnp.where(allowed, jnp.einsum(SCORE_FORM, query_h, key_h) * scaling, -1e+30)
    weights = jnp.where(allowed, jnp.exp(scores - log_total[..., None]), 0.0)
    grad_weights = jnp.einsum(SCORE_FORM, grad_h, value_h)
    grad_scores = rounded(weights * (grad_weights - delta[..., None]))
    grad_value = rounded(jnp.einsum(BACK_FORM, rounded(weights), grad_h))
    grad_query = rounded(jnp.einsum(APPLY_FORM, grad_scores, key_h) * scaling)
    grad_key = rounded(jnp.einsum(BACK_FORM, grad_scores, query_h) * scaling)
    return (grad_query, grad_key, grad_value)

def one_sequence(tokens_s, length, grad_s, w_qkv):
    wide = w_qkv.astype(jnp.float32)
    inputs = tokens_s.astype(jnp.float32)
    stacked = rounded(jnp.einsum('rcd,jdf->jrcf', inputs, wide))
    shape_h = (ROWS, STRIDE, HEADS, HEAD_DIM)
    query_h = stacked[0].reshape(shape_h)
    key_h = stacked[1].reshape(shape_h)
    value_h = stacked[2].reshape(shape_h)
    col_ids = jnp.arange(STRIDE, dtype=jnp.int32)
    row_ids = jnp.arange(ROWS, dtype=jnp.int32)
    key_pos = row_ids[:, None, None] * STRIDE + col_ids[None, None, :]
    same_col = col_ids[None, None, :] == col_ids[None, :, None]
    row_allowed = (col_ids[None, None, :] <= col_ids[None, :, None]) & ((key_pos < length) | same_col)
    row_allowed = row_allowed[:, :, None, :]
    col_key_pos = row_ids[None, None, :] * STRIDE + col_ids[:, None, None]
    column_allowed = (row_ids[None, None, :] < row_ids[None, :, None]) & (col_key_pos < length)
    column_allowed = column_allowed[:, :, None, :]
    row_high, row_total, row_mixed = part_forward(query_h, key_h, value_h, row_allowed)
    col_high, col_total, col_mixed = part_forward(swap_axes(query_h), swap_axes(key_h), swap_axes(value_h), column_allowed)
    col_high = swap_axes(col_high)
    col_total = swap_axes(col_total)
    col_mixed = swap_axes(col_mixed)
    joint = jnp.maximum(row_high, col_high)
    row_factor = jnp.exp(row_high - joint)
    col_factor = jnp.exp(col_high - joint)
    joint_total = row_total * row_factor + col_total * col_factor
    log_total = joint + jnp.log(joint_total)
    combined = (row_mixed * row_factor[..., None] + col_mixed * col_factor[..., None]) / joint_total[..., None]
    attention = combined.reshape(ROWS, STRIDE, D).astype(jnp.bfloat16)
    attention_f = rounded(combined)
    grad_h = grad_s.astype(jnp.float32).reshape(shape_h)
    delta = lax.optimization_barrier(jnp.sum(attention_f * grad_h, axis=-1))
    row_grads = part_back(query_h, key_h, value_h, grad_h, row_allowed, log_total, delta)
    col_grads = part_back(swap_axes(query_h), swap_axes(key_h), swap_axes(value_h), swap_axes(grad_h), column_allowed, swap_axes(log_total), swap_axes(delta))
    row_parts = jnp.stack(row_grads).reshape(3, ROWS, STRIDE, D)
    col_parts = jnp.stack([swap_axes(item) for item in col_grads]).reshape(3, ROWS, STRIDE, D)
    input_grad = jnp.einsum('jrcf,jdf->rcd', row_parts, wide) + jnp.einsum('jrcf,jdf->rcd', col_parts, wide)
    weight_part = jnp.einsum('rcd,jrcf->jdf', inputs, row_parts) + jnp.einsum('rcd,jrcf->jdf', inputs, col_parts)
    return (attention, input_grad.astype(jnp.bfloat16), weight_part)

def reference(tokens, lengths, w_qkv, out_grad):

    def per_sequence(items):
        return one_sequence(items[0], items[1], items[2], w_qkv)
    attention, input_grad, weight_parts = lax.map(per_sequence, (tokens, lengths, out_grad))
    return (attention, input_grad, lax.optimization_barrier(jnp.sum(weight_parts, axis=0)))
```

```python
import functools
import math

import jax
import jax.numpy as jnp
from jax import lax
from jax.experimental import pallas as pl
from jax.experimental.pallas import tpu as pltpu
from jax.sharding import PartitionSpec as P

HEADS = 8
GROUPS = 4
NONE = -1e30
FLOOR = -1e29
FAR = 1 << 20
NT = (((1,), (1,)), ((), ()))
NN = (((1,), (0,)), ((), ()))
TN = (((0,), (0,)), ((), ()))
VMEM_LIMIT = 48 * 1024 * 1024


def dot(left, right, form):
    return lax.dot_general(left, right, form, preferred_element_type=jnp.float32)


def spread(values, first, packed, width):
    zero = jnp.zeros((values.shape[0], width), values.dtype)
    lines = []
    for i in range(packed):
        own = values[:, (first + i) * width : (first + i + 1) * width]
        lines.append(jnp.concatenate([own if j == i else zero for j in range(packed)], axis=1))
    return jnp.concatenate(lines, axis=0)


def tile_lanes(values, times):
    return jnp.concatenate([values] * times, axis=1) if times > 1 else values


def part_stats(query, key, value, grad, mask, packed, store):
    width = key.shape[1] // HEADS
    scaling = 1.0 / math.sqrt(width)
    for first in range(0, HEADS, packed):
        lanes = slice(first * width, (first + packed) * width)
        scores = dot(key[:, lanes], spread(query, first, packed, width), NT) * scaling
        grad_prob = dot(value[:, lanes], spread(grad, first, packed, width), NT)
        scores = jnp.where(mask, scores, NONE)
        highest = jnp.maximum(jnp.max(scores, axis=0, keepdims=True), FLOOR)
        weights = jnp.exp(scores - highest)
        total = jnp.sum(weights, axis=0, keepdims=True)
        product = jnp.sum(weights * grad_prob, axis=0, keepdims=True)
        store(first, highest, total, product)


def part_grads(query, key, value, grad, mask, packed, load, store):
    width = key.shape[1] // HEADS
    scaling = 1.0 / math.sqrt(width)
    count = query.shape[0]
    for first in range(0, HEADS, packed):
        lanes = slice(first * width, (first + packed) * width)
        query_d = spread(query, first, packed, width)
        grad_d = spread(grad, first, packed, width)
        joint, inverse, delta = load(first)
        scores = dot(key[:, lanes], query_d, NT) * scaling
        grad_prob = dot(value[:, lanes], grad_d, NT)
        scores = jnp.where(mask, scores, NONE)
        prob = jnp.exp(scores - joint) * inverse
        grad_score = (prob * (grad_prob - delta)).astype(jnp.bfloat16)
        prob = prob.astype(jnp.bfloat16)
        grad_value = dot(prob, grad_d, NN)
        grad_key = dot(grad_score, query_d, NN) * scaling
        mixed, grad_query = [], []
        for i in range(packed):
            ours = slice(i * count, (i + 1) * count)
            head = slice((first + i) * width, (first + i + 1) * width)
            mixed.append(dot(prob[:, ours], value[:, head], TN))
            grad_query.append(dot(grad_score[:, ours], key[:, head], TN) * scaling)
        store(
            lanes,
            jnp.concatenate(mixed, axis=1),
            jnp.concatenate(grad_query, axis=1),
            grad_key,
            grad_value,
        )


def row_mask(scalars, row, count, packed):
    keys = lax.broadcasted_iota(jnp.int32, (count, count), 0)
    queries = lax.broadcasted_iota(jnp.int32, (count, count), 1)
    limit = scalars[0] - row * count
    allowed = (keys < queries) & (keys < limit) | (keys == queries)
    return tile_lanes(allowed.astype(jnp.int32), packed) > 0


def row_stats_kernel(packed, scalars, query, key, value, grad, stats):
    count = key.shape[1]
    mask = row_mask(scalars, scalars[1] + pl.program_id(0), count, packed)

    def store(first, *items):
        for j, item in enumerate(items):
            stats[0, j : j + 1, first * count : (first + packed) * count] = item

    part_stats(query[0], key[0], value[0], grad[0], mask, packed, store)


def row_grads_kernel(packed, scalars, stats, query, key, value, grad, mixed, g_query, g_key, g_value):
    count = key.shape[1]
    mask = row_mask(scalars, scalars[1] + pl.program_id(0), count, packed)

    def load(first):
        return [stats[0, j : j + 1, first * count : (first + packed) * count] for j in range(3)]

    def store(lanes, mixed_v, query_v, key_v, value_v):
        mixed[0, :, lanes] = mixed_v.astype(mixed.dtype)
        g_query[0, :, lanes] = query_v.astype(g_query.dtype)
        g_key[0, :, lanes] = key_v.astype(g_key.dtype)
        g_value[0, :, lanes] = value_v.astype(g_value.dtype)

    part_grads(query[0], key[0], value[0], grad[0], mask, packed, load, store)


def col_mask(scalars, key_rows, query_rows, column, stride):
    rows = key_rows[...]
    rows = jnp.where(rows * stride + column < scalars[0], rows, FAR)
    times = query_rows.shape[1] // rows.shape[1]
    return tile_lanes(rows, times) < query_rows[0:1, :]


def col_stats_kernel(
    packed, stride, scalars, key_rows, query_rows, query, guest, key, value, grad, guest_grad, stats, crossed
):
    count = 2 * query.shape[1]
    half = query.shape[1]
    for i in range(key.shape[0]):
        column = scalars[1] + pl.program_id(0) * key.shape[0] + i
        mask = col_mask(scalars, key_rows, query_rows, column, stride)

        def store(first, *items):
            lanes = slice(first * count, (first + packed) * count)
            for j, item in enumerate(items):
                stats[i, j : j + 1, lanes] = item
                pieces = []
                for h in range(packed):
                    pieces.append(item[:, h * count + half : (h + 1) * count])
                    pieces.append(item[:, h * count : h * count + half])
                crossed[i, j : j + 1, lanes] = jnp.concatenate(pieces, axis=1)

        query_v = jnp.concatenate([query[i], guest[i]], axis=0)
        grad_v = jnp.concatenate([grad[i], guest_grad[i]], axis=0)
        part_stats(query_v, key[i], value[i], grad_v, mask, packed, store)


def join(parts):
    highs = [jnp.where(total > 0.0, high, NONE) for high, total, _ in parts]
    joint = functools.reduce(jnp.maximum, highs)
    factors = [jnp.exp(high - joint) for high in highs]
    total = sum(part[1] * factor for part, factor in zip(parts, factors))
    product = sum(part[2] * factor for part, factor in zip(parts, factors))
    inverse = jnp.where(total > 0.0, 1.0 / jnp.where(total > 0.0, total, 1.0), 0.0)
    return joint, inverse, product * inverse


def col_grads_kernel(
    packed, stride, scalars, key_rows, query_rows, row_part, own_part, other_part,
    query, guest, key, value, grad, guest_grad,
    final, mixed, guest_mixed, g_query, g_guest, g_key, g_value,
):
    half = query.shape[1]
    count = 2 * half
    for i in range(key.shape[0]):
        column = scalars[1] + pl.program_id(0) * key.shape[0] + i
        mask = col_mask(scalars, key_rows, query_rows, column, stride)

        def load(first):
            lanes = slice(first * count, (first + packed) * count)
            parts = [
                [part[i, j : j + 1, lanes] for j in range(3)]
                for part in (row_part, own_part, other_part)
            ]
            result = join(parts)
            for j in range(3):
                final[i, j : j + 1, lanes] = result[j]
            return result

        def store(lanes, mixed_v, query_v, key_v, value_v):
            mixed[i, :, lanes] = mixed_v[:half].astype(mixed.dtype)
            guest_mixed[i, :, lanes] = mixed_v[half:].astype(mixed.dtype)
            g_query[i, :, lanes] = query_v[:half].astype(g_query.dtype)
            g_guest[i, :, lanes] = query_v[half:].astype(g_query.dtype)
            g_key[i, :, lanes] = key_v.astype(g_key.dtype)
            g_value[i, :, lanes] = value_v.astype(g_value.dtype)

        query_v = jnp.concatenate([query[i], guest[i]], axis=0)
        grad_v = jnp.concatenate([grad[i], guest_grad[i]], axis=0)
        part_grads(query_v, key[i], value[i], grad_v, mask, packed, load, store)


def call(kernel, steps, in_specs, out_specs, out_shapes, flops, operands):
    return pl.pallas_call(
        kernel,
        grid=(steps,),
        in_specs=in_specs,
        out_specs=out_specs,
        out_shape=out_shapes,
        compiler_params=pltpu.CompilerParams(vmem_limit_bytes=VMEM_LIMIT),
        cost_estimate=pl.CostEstimate(flops=flops, bytes_accessed=flops // 1000, transcendentals=0),
    )(*operands)


def block(shape, offset=0):
    rest = (0,) * (len(shape) - 1)
    return pl.BlockSpec(shape, lambda s: (s + offset,) + rest)


def whole(shape):
    return pl.BlockSpec(shape, lambda s: (0,) * len(shape))


SCALARS = pl.BlockSpec(memory_space=pltpu.SMEM)


def row_stats(scalars, query, key, value, grad):
    rows, count, width = query.shape
    packed = max(1, min(HEADS, 256 // count))
    one = block((1, count, width))
    return call(
        functools.partial(row_stats_kernel, packed),
        rows,
        [SCALARS] + [one] * 4,
        block((1, 3, HEADS * count)),
        jax.ShapeDtypeStruct((rows, 3, HEADS * count), jnp.float32),
        4 * rows * count * count * width * 4,
        (scalars, query, key, value, grad),
    )


def row_grads(scalars, stats, query, key, value, grad):
    rows, count, width = query.shape
    packed = max(1, min(HEADS, 256 // count))
    one = block((1, count, width))
    return call(
        functools.partial(row_grads_kernel, packed),
        rows,
        [SCALARS, block((1, 3, HEADS * count))] + [one] * 4,
        [one] * 4,
        [jax.ShapeDtypeStruct(query.shape, jnp.bfloat16)] * 4,
        12 * rows * count * count * width * 4,
        (scalars, stats, query, key, value, grad),
    )


def col_sizes(query, key):
    half = query.shape[1]
    packed = max(1, min(HEADS, 256 // (2 * half)))
    columns = key.shape[0]
    step = 2 if columns % 2 == 0 else 1
    return half, packed, columns, step


def col_stats(scalars, key_rows, query_rows, query, guest, key, value, grad, guest_grad, offset, stride):
    half, packed, columns, step = col_sizes(query, key)
    width = key.shape[2]
    own = block((step, half, width), offset // step)
    visitor = block((step, half, width))
    keys = block((step, key.shape[1], width))
    stat = block((step, 3, HEADS * 2 * half))
    shape = jax.ShapeDtypeStruct((columns, 3, HEADS * 2 * half), jnp.float32)
    return call(
        functools.partial(col_stats_kernel, packed, stride),
        columns // step,
        [SCALARS, whole(key_rows.shape), whole(query_rows.shape), own, visitor, keys, keys, own, visitor],
        [stat, stat],
        [shape, shape],
        4 * columns * key.shape[1] * 2 * half * width * 4,
        (scalars, key_rows, query_rows, query, guest, key, value, grad, guest_grad),
    )


def col_grads(
    scalars, key_rows, query_rows, row_part, own_part, other_part,
    query, guest, key, value, grad, guest_grad, offset, stride,
):
    half, packed, columns, step = col_sizes(query, key)
    width = key.shape[2]
    own = block((step, half, width), offset // step)
    visitor = block((step, half, width))
    keys = block((step, key.shape[1], width))
    stat = block((step, 3, HEADS * 2 * half))
    stat_off = block((step, 3, HEADS * 2 * half), offset // step)
    shape = jax.ShapeDtypeStruct((columns, 3, HEADS * 2 * half), jnp.float32)
    small = jax.ShapeDtypeStruct((columns, half, width), jnp.bfloat16)
    large = jax.ShapeDtypeStruct(key.shape, jnp.bfloat16)
    return call(
        functools.partial(col_grads_kernel, packed, stride),
        columns // step,
        [SCALARS, whole(key_rows.shape), whole(query_rows.shape), stat_off, stat, stat]
        + [own, visitor, keys, keys, own, visitor],
        [stat, visitor, visitor, visitor, visitor, keys, keys],
        [shape, small, small, small, small, large, large],
        12 * columns * key.shape[1] * 2 * half * width * 4,
        (scalars, key_rows, query_rows, row_part, own_part, other_part)
        + (query, guest, key, value, grad, guest_grad),
    )


def product(values, weight):
    return jnp.einsum("...d,df->...f", values, weight, preferred_element_type=jnp.float32)


def product_t(values, weight):
    return jnp.einsum("...f,df->...d", values, weight, preferred_element_type=jnp.float32)


def weight_product(values, grads):
    return jnp.einsum("abd,abf->df", values, grads, preferred_element_type=jnp.float32)


def narrow(values):
    return values.astype(jnp.bfloat16)


def body(tokens, lengths, w_qkv, out_grad):
    seq_count = lax.axis_size("seq")
    seq_index = lax.axis_index("seq")
    chips = seq_count // 2
    chip, core = seq_index // 2, seq_index % 2
    seq_local, row_local, columns, width = tokens.shape
    half_cols = columns // 2
    chip_rows = 2 * row_local
    group = half_cols // GROUPS
    w_q, w_k, w_v = w_qkv[0], w_qkv[1], w_qkv[2]

    def pairs(links):
        return [(2 * a + c, 2 * b + c) for a, b in links for c in (0, 1)]

    swap = [(i, i ^ 1) for i in range(seq_count)]
    up = {k: pairs([(z - 1, z) for z in range(k, chips - 1)]) for k in range(1, chips - 1)}
    down = {k: [(b, a) for a, b in up[k]] for k in up}
    guest_up = pairs([(chips - 2, chips - 1)])
    guest_down = pairs([(chips - 1, chips - 2)])

    def send(values, perm):
        return lax.ppermute(values, "seq", perm)

    def to_columns(values, axis, row_axis):
        mine = lax.dynamic_slice_in_dim(values, core * half_cols, half_cols, axis)
        others = lax.dynamic_slice_in_dim(values, (1 - core) * half_cols, half_cols, axis)
        return jnp.concatenate([mine, send(others, swap)], axis=row_axis)

    def to_rows(values, axis, row_axis):
        mine = lax.slice_in_dim(values, 0, row_local, axis=row_axis)
        others = send(lax.slice_in_dim(values, row_local, chip_rows, axis=row_axis), swap)
        return jnp.where(
            core == 0,
            jnp.concatenate([mine, others], axis=axis),
            jnp.concatenate([others, mine], axis=axis),
        )

    tokens_r, grad_r = tokens[0], out_grad[0]
    limit = lengths[0]
    tokens_c = to_columns(jnp.swapaxes(tokens_r, 0, 1), 0, 1)
    grad_c = to_columns(jnp.swapaxes(grad_r, 0, 1), 0, 1)

    order = (jnp.arange(chip_rows, dtype=jnp.int32) + core * row_local) % chip_rows
    key_ids = []
    for k in range(chips - 2, -1, -1):
        valid = (chip >= k) & (chip <= chips - 2) if k > 0 else chip >= 0
        key_ids.append(jnp.where(valid, (chip - k) * chip_rows + order, FAR))
    key_ids = jnp.concatenate(key_ids)
    query_ids = jnp.concatenate(
        [chip * chip_rows + order, jnp.where(chip == chips - 2, (chip + 1) * chip_rows + order, -1)]
    )
    packed = max(1, min(HEADS, 256 // (2 * chip_rows)))
    lane = min(128, packed * 2 * chip_rows)
    key_rows = jnp.broadcast_to(key_ids[:, None], (key_ids.shape[0], lane))
    query_rows = jnp.broadcast_to(jnp.tile(query_ids, packed)[None], (8, packed * 2 * chip_rows))

    blocks = []
    for g in range(GROUPS):
        held = [tokens_c[g * group : (g + 1) * group]]
        for k in range(1, chips - 1):
            held.append(send(held[-1], up[k]))
        blocks.append(jnp.concatenate(held[::-1], axis=1))

    query_c = narrow(product(tokens_c, w_q))
    guests, guest_grads = [], []
    for g in range(GROUPS):
        guests.append(send(query_c[g * group : (g + 1) * group], guest_down))
        guest_grads.append(send(grad_c[g * group : (g + 1) * group], guest_down))

    query_r, key_r, value_r = (narrow(product(tokens_r, w)) for w in (w_q, w_k, w_v))
    row_scalars = jnp.stack([limit, seq_index * row_local]).astype(jnp.int32)
    row_part = row_stats(row_scalars, query_r, key_r, value_r, grad_r)
    row_part = row_part.reshape(row_local, 3, HEADS, columns).transpose(3, 1, 2, 0)
    row_part = to_columns(row_part, 0, 3)
    row_part = jnp.concatenate([row_part, send(row_part, guest_down)], axis=3)
    row_part = row_part.reshape(half_cols, 3, HEADS * 2 * chip_rows)

    cross = guest_up + guest_down
    finals, mixed_c, w_parts, own_terms = [], [], [], []
    for g in range(GROUPS):
        scalars = jnp.stack([limit, core * half_cols + g * group]).astype(jnp.int32)
        key_g = narrow(product(blocks[g], w_k))
        value_g = narrow(product(blocks[g], w_v))
        operands = (query_c, guests[g], key_g, value_g, grad_c, guest_grads[g], g * group, columns)
        own_part, crossed = col_stats(scalars, key_rows, query_rows, *operands)
        other_part = send(crossed, cross)
        final, mixed, guest_mixed, g_query, g_guest, g_key, g_value = col_grads(
            scalars, key_rows, query_rows, row_part, own_part, other_part, *operands
        )
        finals.append(final)
        mixed_c.append(
            narrow(mixed.astype(jnp.float32) + send(guest_mixed, guest_up).astype(jnp.float32))
        )
        g_query = narrow(g_query.astype(jnp.float32) + send(g_guest, guest_up).astype(jnp.float32))
        terms = product_t(g_key, w_k) + product_t(g_value, w_v)
        moving = None
        for k in range(chips - 2, -1, -1):
            at = (chips - 2 - k) * chip_rows
            term = terms[:, at : at + chip_rows]
            if moving is not None:
                term = term + moving.astype(jnp.float32)
            if k > 0:
                moving = send(narrow(term), down[k])
            else:
                own_terms.append(narrow(term + product_t(g_query, w_q)))
        tokens_g = tokens_c[g * group : (g + 1) * group]
        w_parts.append(
            (
                weight_product(tokens_g, g_query),
                weight_product(blocks[g], g_key),
                weight_product(blocks[g], g_value),
            )
        )

    final = jnp.concatenate(finals, axis=0).reshape(half_cols, 3, HEADS, 2 * chip_rows)
    final = to_rows(final[..., :chip_rows], 0, 3)
    final = final.transpose(3, 1, 2, 0).reshape(row_local, 3, HEADS * columns)
    mixed_r, g_query_r, g_key_r, g_value_r = row_grads(
        row_scalars, final, query_r, key_r, value_r, grad_r
    )
    mixed_b = jnp.swapaxes(to_rows(jnp.concatenate(mixed_c, axis=0), 0, 1), 0, 1)
    attention = narrow(mixed_r.astype(jnp.float32) + mixed_b.astype(jnp.float32))
    terms_b = jnp.swapaxes(to_rows(jnp.concatenate(own_terms, axis=0), 0, 1), 0, 1)
    input_sum = (
        product_t(g_query_r, w_q) + product_t(g_key_r, w_k) + product_t(g_value_r, w_v)
    ) + terms_b.astype(jnp.float32)
    input_grad = narrow(input_sum)

    shares = []
    for j, grads in enumerate((g_query_r, g_key_r, g_value_r)):
        part = weight_product(tokens_r, grads)
        for item in w_parts:
            part = part + item[j]
        part = narrow(part).reshape(chips, 2, -1, width)
        mine = lax.dynamic_index_in_dim(part, core, 1, keepdims=False)
        others = lax.dynamic_index_in_dim(part, 1 - core, 1, keepdims=False)
        shares.append(narrow(mine.astype(jnp.float32) + send(others, swap).astype(jnp.float32)))
    share = jnp.stack(shares)
    share = lax.psum_scatter(share, "dp", scatter_dimension=3, tiled=True)
    rings = [[2 * z + c for z in range(chips)] for c in (0, 1)]
    share = lax.psum_scatter(share, "seq", scatter_dimension=1, axis_index_groups=rings, tiled=True)
    w_grads = share[:, 0].astype(jnp.float32)
    return (attention[None], input_grad[None], w_grads)


def solution(mesh):
    in_specs = (P("dp", "seq", None, None), P("dp"), P(), P("dp", "seq", None, None))
    out_specs = (P("dp", "seq", None, None), P("dp", "seq", None, None), P(None, "seq", "dp"))
    return jax.shard_map(body, mesh=mesh, in_specs=in_specs, out_specs=out_specs, check_vma=False)
```

```python
import functools
import math

import jax
import jax.numpy as jnp
from jax import lax
from jax.experimental import pallas as pl
from jax.experimental.pallas import tpu as pltpu
from jax.sharding import PartitionSpec as P

HEADS = 8
ROW_STEP = 4
COL_STEP = 8
TILE = 256
GROUPS = 4
NONE = -1e30
FLOOR = -1e29
FAR = 1 << 20
NT = (((1,), (1,)), ((), ()))
NN = (((1,), (0,)), ((), ()))
TN = (((0,), (0,)), ((), ()))
VMEM_LIMIT = 48 * 1024 * 1024


def dot(left, right, form):
    return lax.dot_general(left, right, form, preferred_element_type=jnp.float32)


def spread(values, first, packed, width):
    zero = jnp.zeros((values.shape[0], width), values.dtype)
    lines = []
    for i in range(packed):
        own = values[:, (first + i) * width : (first + i + 1) * width]
        lines.append(jnp.concatenate([own if j == i else zero for j in range(packed)], axis=1))
    return jnp.concatenate(lines, axis=0)


def tile_lanes(values, times):
    return jnp.concatenate([values] * times, axis=1) if times > 1 else values


def part_stats(query, key, value, grad, mask, packed, store):
    width = key.shape[1] // HEADS
    scaling = 1.0 / math.sqrt(width)
    for first in range(0, HEADS, packed):
        lanes = slice(first * width, (first + packed) * width)
        scores = dot(key[:, lanes], spread(query, first, packed, width), NT) * scaling
        grad_prob = dot(value[:, lanes], spread(grad, first, packed, width), NT)
        scores = jnp.where(mask, scores, NONE)
        highest = jnp.maximum(jnp.max(scores, axis=0, keepdims=True), FLOOR)
        weights = jnp.exp(scores - highest)
        total = jnp.sum(weights, axis=0, keepdims=True)
        product = jnp.sum(weights * grad_prob, axis=0, keepdims=True)
        store(first, highest, total, product)


def part_grads(query, key, value, grad, mask, packed, load, store):
    width = key.shape[1] // HEADS
    scaling = 1.0 / math.sqrt(width)
    count = query.shape[0]
    for first in range(0, HEADS, packed):
        lanes = slice(first * width, (first + packed) * width)
        query_d = spread(query, first, packed, width)
        grad_d = spread(grad, first, packed, width)
        joint, inverse, delta = load(first)
        scores = dot(key[:, lanes], query_d, NT) * scaling
        grad_prob = dot(value[:, lanes], grad_d, NT)
        scores = jnp.where(mask, scores, NONE)
        prob = jnp.exp(scores - joint) * inverse
        grad_score = (prob * (grad_prob - delta)).astype(jnp.bfloat16)
        prob = prob.astype(jnp.bfloat16)
        grad_value = dot(prob, grad_d, NN)
        grad_key = dot(grad_score, query_d, NN) * scaling
        mixed, grad_query = [], []
        prob_t, score_t = prob.T, grad_score.T
        for i in range(packed):
            ours = slice(i * count, (i + 1) * count)
            head = slice((first + i) * width, (first + i + 1) * width)
            mixed.append(dot(prob_t[ours], value[:, head], NN))
            grad_query.append(dot(score_t[ours], key[:, head], NN) * scaling)
        store(
            lanes,
            jnp.concatenate(mixed, axis=1),
            jnp.concatenate(grad_query, axis=1),
            grad_key,
            grad_value,
        )


def row_mask(scalars, row, count, packed):
    keys = lax.broadcasted_iota(jnp.int32, (count, count), 0)
    queries = lax.broadcasted_iota(jnp.int32, (count, count), 1)
    limit = scalars[0] - row * count
    allowed = (keys < queries) & (keys < limit) | (keys == queries)
    return tile_lanes(allowed.astype(jnp.int32), packed) > 0


def thirds(ref, i):
    width = ref.shape[2] // 3
    return [ref[i, :, j * width : (j + 1) * width] for j in range(3)]


def halves(ref, i):
    width = ref.shape[2] // 2
    return ref[i, :, :width], ref[i, :, width:]


def row_stats_kernel(packed, scalars, qkv, grad, stats):
    count = qkv.shape[1]
    for i in range(qkv.shape[0]):
        mask = row_mask(scalars, scalars[1] + pl.program_id(0) * qkv.shape[0] + i, count, packed)

        def store(first, *items):
            for j, item in enumerate(items):
                stats[i, j : j + 1, first * count : (first + packed) * count] = item

        part_stats(*thirds(qkv, i), grad[i], mask, packed, store)


def row_grads_kernel(packed, scalars, stats, qkv, grad, mixed, g_qkv):
    count = qkv.shape[1]
    width = grad.shape[2]
    for i in range(qkv.shape[0]):
        mask = row_mask(scalars, scalars[1] + pl.program_id(0) * qkv.shape[0] + i, count, packed)

        def load(first):
            return [stats[i, j : j + 1, first * count : (first + packed) * count] for j in range(3)]

        def store(lanes, mixed_v, query_v, key_v, value_v):
            mixed[i, :, lanes] = mixed_v.astype(mixed.dtype)
            for j, item in enumerate((query_v, key_v, value_v)):
                place = slice(j * width + lanes.start, j * width + lanes.stop)
                g_qkv[i, :, place] = item.astype(g_qkv.dtype)

        part_grads(*thirds(qkv, i), grad[i], mask, packed, load, store)


def col_mask(scalars, key_rows, query_rows, column, stride):
    rows = key_rows[...]
    rows = jnp.where(rows * stride + column < scalars[0], rows, FAR)
    times = query_rows.shape[1] // rows.shape[1]
    return tile_lanes(rows, times) < query_rows[0:1, :]


def col_stats_kernel(
    packed, stride, scalars, key_rows, query_rows, query, guest, grad, guest_grad, weight, *rest
):
    *held, stats, crossed, kv, inputs = rest
    count = 2 * query.shape[1]
    half = query.shape[1]
    for b, item in enumerate(held):
        inputs[:, b * half : (b + 1) * half, :] = item[...]
    columns, keys, width = inputs.shape
    flat = inputs[...].reshape(columns * keys, width)
    for at in range(0, 2 * width, TILE):
        part = dot(flat, weight[:, at : at + TILE], NN).astype(kv.dtype)
        kv[:, :, at : at + TILE] = part.reshape(columns, keys, TILE)
    for i in range(kv.shape[0]):
        column = scalars[1] + pl.program_id(0) * kv.shape[0] + i
        mask = col_mask(scalars, key_rows, query_rows, column, stride)

        def store(first, *items):
            lanes = slice(first * count, (first + packed) * count)
            for j, item in enumerate(items):
                stats[i, j : j + 1, lanes] = item
                pieces = []
                for h in range(packed):
                    pieces.append(item[:, h * count + half : (h + 1) * count])
                    pieces.append(item[:, h * count : h * count + half])
                crossed[i, j : j + 1, lanes] = jnp.concatenate(pieces, axis=1)

        query_v = jnp.concatenate([query[i], guest[i]], axis=0)
        grad_v = jnp.concatenate([grad[i], guest_grad[i]], axis=0)
        part_stats(query_v, *halves(kv, i), grad_v, mask, packed, store)


def join(parts):
    highs = [jnp.where(total > 0.0, high, NONE) for high, total, _ in parts]
    joint = functools.reduce(jnp.maximum, highs)
    factors = [jnp.exp(high - joint) for high in highs]
    total = sum(part[1] * factor for part, factor in zip(parts, factors))
    product = sum(part[2] * factor for part, factor in zip(parts, factors))
    inverse = jnp.where(total > 0.0, 1.0 / jnp.where(total > 0.0, total, 1.0), 0.0)
    return joint, inverse, product * inverse


def col_grads_kernel(
    packed, stride, scalars, key_rows, query_rows, row_part, own_part, other_part,
    query, guest, kv, grad, guest_grad, weight,
    final, mixed, g_query, back, g_kv, *terms,
):
    half = query.shape[1]
    count = 2 * half
    width = query.shape[2]
    for i in range(kv.shape[0]):
        column = scalars[1] + pl.program_id(0) * kv.shape[0] + i
        mask = col_mask(scalars, key_rows, query_rows, column, stride)

        def load(first):
            lanes = slice(first * count, (first + packed) * count)
            parts = [
                [part[i, j : j + 1, lanes] for j in range(3)]
                for part in (row_part, own_part, other_part)
            ]
            result = join(parts)
            for j in range(3):
                final[i, j : j + 1, lanes] = result[j]
            return result

        def store(lanes, mixed_v, query_v, key_v, value_v):
            mixed[i, :, lanes] = mixed_v[:half].astype(mixed.dtype)
            g_query[i, :, lanes] = query_v[:half].astype(g_query.dtype)
            second = slice(width + lanes.start, width + lanes.stop)
            back[i, :, lanes] = mixed_v[half:].astype(back.dtype)
            back[i, :, second] = query_v[half:].astype(back.dtype)
            g_kv[i, :, lanes] = key_v.astype(g_kv.dtype)
            g_kv[i, :, second] = value_v.astype(g_kv.dtype)

        query_v = jnp.concatenate([query[i], guest[i]], axis=0)
        grad_v = jnp.concatenate([grad[i], guest_grad[i]], axis=0)
        part_grads(query_v, *halves(kv, i), grad_v, mask, packed, load, store)

    columns, keys, _ = g_kv.shape
    flat = g_kv[...].reshape(columns * keys, 2 * width)
    for at in range(0, width, TILE):
        part = dot(flat, weight[:, at : at + TILE], NN).astype(g_kv.dtype).reshape(columns, keys, TILE)
        for b, term in enumerate(terms):
            term[:, :, at : at + TILE] = part[:, b * half : (b + 1) * half]


def call(kernel, steps, in_specs, out_specs, out_shapes, flops, operands):
    return pl.pallas_call(
        kernel,
        grid=(steps,),
        in_specs=in_specs,
        out_specs=out_specs,
        out_shape=out_shapes,
        compiler_params=pltpu.CompilerParams(vmem_limit_bytes=VMEM_LIMIT),
        cost_estimate=pl.CostEstimate(flops=flops, bytes_accessed=flops // 1000, transcendentals=0),
    )(*operands)


def block(shape, offset=0):
    rest = (0,) * (len(shape) - 1)
    return pl.BlockSpec(shape, lambda s: (s + offset,) + rest)


def whole(shape):
    return pl.BlockSpec(shape, lambda s: (0,) * len(shape))


SCALARS = pl.BlockSpec(memory_space=pltpu.SMEM)


def row_stats(scalars, qkv, grad):
    rows, count, width = grad.shape
    packed = max(1, min(HEADS, 256 // count))
    step = math.gcd(rows, ROW_STEP)
    return call(
        functools.partial(row_stats_kernel, packed),
        rows // step,
        [SCALARS, block((step, count, 3 * width)), block((step, count, width))],
        block((step, 3, HEADS * count)),
        jax.ShapeDtypeStruct((rows, 3, HEADS * count), jnp.float32),
        4 * rows * count * count * width * 4,
        (scalars, qkv, grad),
    )


def row_grads(scalars, stats, qkv, grad):
    rows, count, width = grad.shape
    packed = max(1, min(HEADS, 256 // count))
    step = math.gcd(rows, ROW_STEP)
    one, three = block((step, count, width)), block((step, count, 3 * width))
    return call(
        functools.partial(row_grads_kernel, packed),
        rows // step,
        [SCALARS, block((step, 3, HEADS * count)), three, one],
        [one, three],
        [jax.ShapeDtypeStruct(x.shape, jnp.bfloat16) for x in (grad, qkv)],
        12 * rows * count * count * width * 4,
        (scalars, stats, qkv, grad),
    )


def col_sizes(query):
    columns, half, width = query.shape
    packed = max(1, min(HEADS, 256 // (2 * half)))
    return half, packed, columns, math.gcd(columns, COL_STEP), width


def col_stats(scalars, key_rows, query_rows, query, guest, grad, guest_grad, weight, held, stride):
    half, packed, columns, step, width = col_sizes(query)
    keys = half * len(held)
    own = block((step, half, width))
    stat = block((step, 3, HEADS * 2 * half))
    shape = jax.ShapeDtypeStruct((columns, 3, HEADS * 2 * half), jnp.float32)
    large = jax.ShapeDtypeStruct((columns, keys, 2 * width), jnp.bfloat16)
    joined = jax.ShapeDtypeStruct((columns, keys, width), jnp.bfloat16)
    return call(
        functools.partial(col_stats_kernel, packed, stride),
        columns // step,
        [SCALARS, whole(key_rows.shape), whole(query_rows.shape)]
        + [own, own, own, own, whole(weight.shape)]
        + [own] * len(held),
        [stat, stat, block((step, keys, 2 * width)), block((step, keys, width))],
        [shape, shape, large, joined],
        4 * columns * keys * width * (2 * half * 4 + width),
        (scalars, key_rows, query_rows, query, guest, grad, guest_grad, weight, *held),
    )


def col_grads(
    scalars, key_rows, query_rows, row_part, own_part, other_part,
    query, guest, kv, grad, guest_grad, weight, offset, stride,
):
    half, packed, columns, step, width = col_sizes(query)
    keys = kv.shape[1]
    blocks = keys // half
    own = block((step, half, width))
    both = block((step, half, 2 * width))
    pair = block((step, keys, 2 * width))
    stat = block((step, 3, HEADS * 2 * half))
    stat_off = block((step, 3, HEADS * 2 * half), offset // step)
    shape = jax.ShapeDtypeStruct((columns, 3, HEADS * 2 * half), jnp.float32)
    small = jax.ShapeDtypeStruct((columns, half, width), jnp.bfloat16)
    twice = jax.ShapeDtypeStruct((columns, half, 2 * width), jnp.bfloat16)
    large = jax.ShapeDtypeStruct(kv.shape, jnp.bfloat16)
    return call(
        functools.partial(col_grads_kernel, packed, stride),
        columns // step,
        [SCALARS, whole(key_rows.shape), whole(query_rows.shape), stat_off, stat, stat]
        + [own, own, pair, own, own, whole(weight.shape)],
        [stat, own, own, both, pair] + [own] * blocks,
        [shape, small, small, twice, large] + [small] * blocks,
        4 * columns * keys * width * (6 * half * 4 + width),
        (scalars, key_rows, query_rows, row_part, own_part, other_part)
        + (query, guest, kv, grad, guest_grad, weight),
    )


def product(values, weight):
    return jnp.einsum("...d,df->...f", values, weight, preferred_element_type=jnp.float32)


def product_t(values, weight):
    return jnp.einsum("...f,df->...d", values, weight, preferred_element_type=jnp.float32)


def weight_product(values, grads):
    return jnp.einsum("abd,abf->df", values, grads, preferred_element_type=jnp.float32)


def narrow(values):
    return values.astype(jnp.bfloat16)


def body(tokens, lengths, w_qkv, out_grad):
    seq_count = lax.axis_size("seq")
    seq_index = lax.axis_index("seq")
    chips = seq_count // 2
    chip, core = seq_index // 2, seq_index % 2
    seq_local, row_local, columns, width = tokens.shape
    half_cols = columns // 2
    chip_rows = 2 * row_local
    group = half_cols // GROUPS
    w_q = w_qkv[0]
    w_kv = jnp.concatenate([w_qkv[1], w_qkv[2]], axis=1)
    w_all = jnp.concatenate([w_q, w_kv], axis=1)
    w_kv_t = jnp.concatenate([w_qkv[1].T, w_qkv[2].T], axis=0)

    def pairs(links):
        return [(2 * a + c, 2 * b + c) for a, b in links for c in (0, 1)]

    swap = [(i, i ^ 1) for i in range(seq_count)]
    up = {k: pairs([(z - 1, z) for z in range(k, chips - 1)]) for k in range(1, chips - 1)}
    down = {k: [(b, a) for a, b in up[k]] for k in up}
    guest_up = pairs([(chips - 2, chips - 1)])
    guest_down = pairs([(chips - 1, chips - 2)])

    def send(values, perm):
        return lax.ppermute(values, "seq", perm)

    def to_columns(values, axis, row_axis):
        mine = lax.dynamic_slice_in_dim(values, core * half_cols, half_cols, axis)
        others = lax.dynamic_slice_in_dim(values, (1 - core) * half_cols, half_cols, axis)
        return jnp.concatenate([mine, send(others, swap)], axis=row_axis)

    def to_rows(values, axis, row_axis):
        mine = lax.slice_in_dim(values, 0, row_local, axis=row_axis)
        others = send(lax.slice_in_dim(values, row_local, chip_rows, axis=row_axis), swap)
        return jnp.where(
            core == 0,
            jnp.concatenate([mine, others], axis=axis),
            jnp.concatenate([others, mine], axis=axis),
        )

    tokens_r, grad_r = tokens[0], out_grad[0]
    limit = lengths[0]


    def by_group(values):
        values = jnp.swapaxes(values, 0, 1)
        mine = lax.dynamic_slice_in_dim(values, core * half_cols, half_cols, 0)
        others = lax.dynamic_slice_in_dim(values, (1 - core) * half_cols, half_cols, 0)
        items = []
        for g in range(GROUPS):
            part = slice(g * group, (g + 1) * group)
            items.append(jnp.concatenate([mine[part], send(others[part], swap)], axis=1))
        return items

    tokens_c, grad_c = by_group(tokens_r), by_group(grad_r)

    order = (jnp.arange(chip_rows, dtype=jnp.int32) + core * row_local) % chip_rows
    key_ids = []
    for k in range(chips - 2, -1, -1):
        valid = (chip >= k) & (chip <= chips - 2) if k > 0 else chip >= 0
        key_ids.append(jnp.where(valid, (chip - k) * chip_rows + order, FAR))
    key_ids = jnp.concatenate(key_ids)
    query_ids = jnp.concatenate(
        [chip * chip_rows + order, jnp.where(chip == chips - 2, (chip + 1) * chip_rows + order, -1)]
    )
    packed = max(1, min(HEADS, 256 // (2 * chip_rows)))
    lane = min(128, packed * 2 * chip_rows)
    key_rows = jnp.broadcast_to(key_ids[:, None], (key_ids.shape[0], lane))
    query_rows = jnp.broadcast_to(jnp.tile(query_ids, packed)[None], (8, packed * 2 * chip_rows))

    hops = chips - 2
    live = dict(tokens_c=tokens_c, grad_c=grad_c, tokens_r=tokens_r, grad_r=grad_r)
    live["held"] = [[tokens_c[g]] for g in range(GROUPS)]
    row_scalars = jnp.stack([limit, seq_index * row_local]).astype(jnp.int32)
    cross = guest_up + guest_down
    names = ("guest", "guest_grad", "kv", "own", "other", "final", "mixed", "query", "terms")
    names += ("back", "moving", "swapped", "w_parts", "query_c")
    live.update({name: [None] * GROUPS for name in names})

    def scalars_of(g):
        return jnp.stack([limit, core * half_cols + g * group]).astype(jnp.int32)

    def step(g, s):
        if 0 <= s < hops:
            live["held"][g].append(send(live["held"][g][-1], up[s + 1]))
        if s == max(hops - 2, 0):
            live["query_c"][g] = narrow(product(live["tokens_c"][g], w_q))
        if s == hops - 1:
            query, grad = live["query_c"][g], live["grad_c"][g]
            if g > 0:
                query, grad, live["crossed"] = lax.optimization_barrier((query, grad, live["crossed"]))
            live["guest"][g] = send(query, guest_down)
            live["guest_grad"][g] = send(grad, guest_down)
        if s == hops:
            live["own"][g], crossed, live["kv"][g], live["held"][g] = col_stats(
                scalars_of(g), key_rows, query_rows,
                live["query_c"][g], live["guest"][g], live["grad_c"][g], live["guest_grad"][g],
                w_kv, live["held"][g][::-1], columns
            )
            live["crossed"] = crossed
            live["other"][g] = send(crossed, cross)
        if s == hops + 1:
            row_part = live["row_part"]
            if g + 1 < GROUPS:
                row_part, live["own"][g + 1] = lax.optimization_barrier((row_part, live["own"][g + 1]))
            final, mixed, g_query, back, g_kv, *terms = col_grads(
                scalars_of(g), key_rows, query_rows, row_part, live["own"][g], live["other"][g],
                live["query_c"][g], live["guest"][g], live["kv"][g], live["grad_c"][g],
                live["guest_grad"][g], w_kv_t, g * group, columns
            )
            live["final"][g], live["mixed"][g], live["query"][g] = final, mixed, g_query
            live["kv"][g], live["back"][g], live["terms"][g] = g_kv, back, terms
        if s == hops + 2:
            back = live["back"][g]
            if g + 2 < GROUPS:
                back, live["crossed"] = lax.optimization_barrier((back, live["crossed"]))
            live["back"][g] = send(back, guest_up)
        if s == hops + 3:
            back = live["back"][g]
            live["mixed"][g] = narrow(
                live["mixed"][g].astype(jnp.float32) + back[..., :width].astype(jnp.float32)
            )
            live["query"][g] = narrow(
                live["query"][g].astype(jnp.float32) + back[..., width:].astype(jnp.float32)
            )
            live["swapped"][g] = send(live["mixed"][g][:, row_local:], swap)
            live["w_parts"][g] = [
                narrow(weight_product(live["tokens_c"][g], live["query"][g])),
                narrow(weight_product(live["held"][g], live["kv"][g])),
            ]
        if hops + 2 <= s <= 2 * hops + 2:
            k = 2 * hops + 2 - s
            term = live["terms"][g][hops - k]
            if k < hops:
                term = term.astype(jnp.float32) + live["moving"][g].astype(jnp.float32)
            if k > 0:
                live["moving"][g] = send(narrow(term), down[k])
            else:
                own = narrow(term + product_t(live["query"][g], w_q))
                live["moving"][g] = (own[:, :row_local], send(own[:, row_local:], swap))

    for t in range(GROUPS + 2 * hops + 2):
        if t == 0:
            live["rows"] = narrow(product(live["tokens_r"], w_all))
        if t == 1:
            part = row_stats(row_scalars, live["rows"], live["grad_r"])
            part = part.reshape(row_local, 3, HEADS, columns).transpose(3, 1, 2, 0)
            part = to_columns(part, 0, 3)
            part = jnp.concatenate([part, send(part, guest_down)], axis=3)
            live["row_part"] = part.reshape(half_cols, 3, HEADS * 2 * chip_rows)
        if t == GROUPS + hops + 1:
            final = jnp.concatenate(live["final"], axis=0).reshape(half_cols, 3, HEADS, 2 * chip_rows)
            final = to_rows(final[..., :chip_rows], 0, 3)
            final = final.transpose(3, 1, 2, 0).reshape(row_local, 3, HEADS * columns)
            live["row_grads"] = row_grads(row_scalars, final, live["rows"], live["grad_r"])
        if t == GROUPS + hops + 2:
            live["w_row"] = weight_product(live["tokens_r"], live["row_grads"][1])
        for g in sorted(range(GROUPS), key=lambda g: t - g != hops):
            step(g, t - g)
        live = lax.optimization_barrier(live)

    def assemble(mine, others):
        mine, others = jnp.concatenate(mine, axis=0), jnp.concatenate(others, axis=0)
        joined = jnp.where(
            core == 0,
            jnp.concatenate([mine, others], axis=0),
            jnp.concatenate([others, mine], axis=0),
        )
        return jnp.swapaxes(joined, 0, 1).astype(jnp.float32)

    mixed_r, row_g = live["row_grads"]
    mixed_b = assemble([item[:, :row_local] for item in live["mixed"]], live["swapped"])
    attention = narrow(mixed_r.astype(jnp.float32) + mixed_b)
    terms_b = assemble(*zip(*live["moving"]))
    input_grad = narrow(product_t(row_g, w_all) + terms_b)

    shares = []
    for j in range(3):
        place = slice(j * width, (j + 1) * width)
        total = live["w_row"][:, place]
        for first, second in live["w_parts"]:
            part = first if j == 0 else second[:, (j - 1) * width : j * width]
            total = total + part.astype(jnp.float32)
        total = narrow(total).reshape(chips, 2, width // seq_count, width)
        mine = lax.dynamic_index_in_dim(total, core, 1, keepdims=False)
        others = lax.dynamic_index_in_dim(total, 1 - core, 1, keepdims=False)
        shares.append(narrow(mine.astype(jnp.float32) + send(others, swap).astype(jnp.float32)))
    share = jnp.stack(shares)
    share = lax.psum_scatter(share, "dp", scatter_dimension=3, tiled=True)
    rings = [[2 * z + c for z in range(chips)] for c in (0, 1)]
    share = lax.psum_scatter(share, "seq", scatter_dimension=1, axis_index_groups=rings, tiled=True)
    w_grads = share[:, 0].astype(jnp.float32)
    return (attention[None], input_grad[None], w_grads)


def solution(mesh):
    in_specs = (P("dp", "seq", None, None), P("dp"), P(), P("dp", "seq", None, None))
    out_specs = (P("dp", "seq", None, None), P("dp", "seq", None, None), P(None, "seq", "dp"))
    return jax.shard_map(body, mesh=mesh, in_specs=in_specs, out_specs=out_specs, check_vma=False)
```

```python
import functools
import math

import jax
import jax.numpy as jnp
from jax import lax
from jax.experimental import pallas as pl
from jax.experimental.pallas import tpu as pltpu
from jax.sharding import PartitionSpec as P

HEADS = 8
ROW_STEP = 4
COL_STEP = 8
TILE = 256
GROUPS = 4
NONE = -1e30
FLOOR = -1e29
FAR = 1 << 20
NT = (((1,), (1,)), ((), ()))
NN = (((1,), (0,)), ((), ()))
TN = (((0,), (0,)), ((), ()))
VMEM_LIMIT = 48 * 1024 * 1024


def dot(left, right, form):
    return lax.dot_general(left, right, form, preferred_element_type=jnp.float32)


def spread(values, first, packed, width):
    zero = jnp.zeros((values.shape[0], width), values.dtype)
    lines = []
    for i in range(packed):
        own = values[:, (first + i) * width : (first + i + 1) * width]
        lines.append(jnp.concatenate([own if j == i else zero for j in range(packed)], axis=1))
    return jnp.concatenate(lines, axis=0)


def tile_lanes(values, times):
    return jnp.concatenate([values] * times, axis=1) if times > 1 else values


def part_stats(query, key, value, grad, mask, packed, store):
    width = key.shape[1] // HEADS
    scaling = 1.0 / math.sqrt(width)
    for first in range(0, HEADS, packed):
        lanes = slice(first * width, (first + packed) * width)
        scores = dot(key[:, lanes], spread(query, first, packed, width), NT) * scaling
        grad_prob = dot(value[:, lanes], spread(grad, first, packed, width), NT)
        scores = jnp.where(mask, scores, NONE)
        highest = jnp.maximum(jnp.max(scores, axis=0, keepdims=True), FLOOR)
        weights = jnp.exp(scores - highest)
        total = jnp.sum(weights, axis=0, keepdims=True)
        product = jnp.sum(weights * grad_prob, axis=0, keepdims=True)
        store(first, highest, total, product)


def part_grads(query, key, value, grad, mask, packed, load, store):
    width = key.shape[1] // HEADS
    scaling = 1.0 / math.sqrt(width)
    count = query.shape[0]
    for first in range(0, HEADS, packed):
        lanes = slice(first * width, (first + packed) * width)
        query_d = spread(query, first, packed, width)
        grad_d = spread(grad, first, packed, width)
        joint, inverse, delta = load(first)
        scores = dot(key[:, lanes], query_d, NT) * scaling
        grad_prob = dot(value[:, lanes], grad_d, NT)
        scores = jnp.where(mask, scores, NONE)
        prob = jnp.exp(scores - joint) * inverse
        grad_score = (prob * (grad_prob - delta)).astype(jnp.bfloat16)
        prob = prob.astype(jnp.bfloat16)
        grad_value = dot(prob, grad_d, NN)
        grad_key = dot(grad_score, query_d, NN) * scaling
        mixed, grad_query = [], []
        prob_t, score_t = prob.T, grad_score.T
        for i in range(packed):
            ours = slice(i * count, (i + 1) * count)
            head = slice((first + i) * width, (first + i + 1) * width)
            mixed.append(dot(prob_t[ours], value[:, head], NN))
            grad_query.append(dot(score_t[ours], key[:, head], NN) * scaling)
        store(
            lanes,
            jnp.concatenate(mixed, axis=1),
            jnp.concatenate(grad_query, axis=1),
            grad_key,
            grad_value,
        )


def row_mask(scalars, row, count, packed):
    keys = lax.broadcasted_iota(jnp.int32, (count, count), 0)
    queries = lax.broadcasted_iota(jnp.int32, (count, count), 1)
    limit = scalars[0] - row * count
    allowed = (keys < queries) & (keys < limit) | (keys == queries)
    return tile_lanes(allowed.astype(jnp.int32), packed) > 0


def thirds(ref, i):
    width = ref.shape[2] // 3
    return [ref[i, :, j * width : (j + 1) * width] for j in range(3)]


def halves(ref, i):
    width = ref.shape[2] // 2
    return ref[i, :, :width], ref[i, :, width:]


def row_stats_kernel(packed, scalars, qkv, grad, stats):
    count = qkv.shape[1]
    for i in range(qkv.shape[0]):
        mask = row_mask(scalars, scalars[1] + pl.program_id(0) * qkv.shape[0] + i, count, packed)

        def store(first, *items):
            for j, item in enumerate(items):
                stats[i, j : j + 1, first * count : (first + packed) * count] = item

        part_stats(*thirds(qkv, i), grad[i], mask, packed, store)


def row_grads_kernel(packed, scalars, stats, qkv, grad, mixed, g_qkv):
    count = qkv.shape[1]
    width = grad.shape[2]
    for i in range(qkv.shape[0]):
        mask = row_mask(scalars, scalars[1] + pl.program_id(0) * qkv.shape[0] + i, count, packed)

        def load(first):
            return [stats[i, j : j + 1, first * count : (first + packed) * count] for j in range(3)]

        def store(lanes, mixed_v, query_v, key_v, value_v):
            mixed[i, :, lanes] = mixed_v.astype(mixed.dtype)
            for j, item in enumerate((query_v, key_v, value_v)):
                place = slice(j * width + lanes.start, j * width + lanes.stop)
                g_qkv[i, :, place] = item.astype(g_qkv.dtype)

        part_grads(*thirds(qkv, i), grad[i], mask, packed, load, store)


def col_mask(scalars, key_rows, query_rows, column, stride):
    rows = key_rows[...]
    rows = jnp.where(rows * stride + column < scalars[0], rows, FAR)
    times = query_rows.shape[1] // rows.shape[1]
    return tile_lanes(rows, times) < query_rows[0:1, :]


def col_stats_kernel(
    packed, stride, scalars, key_rows, query_rows, query, guest, grad, key_weight, value_weight, *rest
):
    *held, stats, crossed, kv, inputs = rest
    count = 2 * query.shape[1]
    half = query.shape[1]
    for b, item in enumerate(held):
        inputs[:, b * half : (b + 1) * half, :] = item[...]
    columns, keys, width = inputs.shape
    flat = inputs[...].reshape(columns * keys, width)
    for j, weight in enumerate((key_weight, value_weight)):
        for at in range(0, width, TILE):
            part = dot(flat, weight[0, :, at : at + TILE], NN).astype(kv.dtype)
            kv[:, :, j * width + at : j * width + at + TILE] = part.reshape(columns, keys, TILE)
    for i in range(kv.shape[0]):
        column = scalars[1] + pl.program_id(0) * kv.shape[0] + i
        mask = col_mask(scalars, key_rows, query_rows, column, stride)

        def store(first, *items):
            lanes = slice(first * count, (first + packed) * count)
            for j, item in enumerate(items):
                stats[i, j : j + 1, lanes] = item
                pieces = []
                for h in range(packed):
                    pieces.append(item[:, h * count + half : (h + 1) * count])
                    pieces.append(item[:, h * count : h * count + half])
                crossed[i, j : j + 1, lanes] = jnp.concatenate(pieces, axis=1)

        query_v = jnp.concatenate([query[i], guest[i, :, :width]], axis=0)
        grad_v = jnp.concatenate([grad[i], guest[i, :, width:]], axis=0)
        part_stats(query_v, *halves(kv, i), grad_v, mask, packed, store)


def join(parts):
    highs = [jnp.where(total > 0.0, high, NONE) for high, total, _ in parts]
    joint = functools.reduce(jnp.maximum, highs)
    factors = [jnp.exp(high - joint) for high in highs]
    total = sum(part[1] * factor for part, factor in zip(parts, factors))
    product = sum(part[2] * factor for part, factor in zip(parts, factors))
    inverse = jnp.where(total > 0.0, 1.0 / jnp.where(total > 0.0, total, 1.0), 0.0)
    return joint, inverse, product * inverse


def col_grads_kernel(
    packed, stride, scalars, key_rows, query_rows, row_part, own_part, other_part,
    query, guest, kv, grad, key_weight, value_weight,
    final, mixed, g_query, back, g_kv, *terms,
):
    half = query.shape[1]
    count = 2 * half
    width = query.shape[2]
    for i in range(kv.shape[0]):
        column = scalars[1] + pl.program_id(0) * kv.shape[0] + i
        mask = col_mask(scalars, key_rows, query_rows, column, stride)

        def load(first):
            lanes = slice(first * count, (first + packed) * count)
            parts = [
                [part[i, j : j + 1, lanes] for j in range(3)]
                for part in (row_part, own_part, other_part)
            ]
            result = join(parts)
            for j in range(3):
                final[i, j : j + 1, lanes] = result[j]
            return result

        def store(lanes, mixed_v, query_v, key_v, value_v):
            mixed[i, :, lanes] = mixed_v[:half].astype(mixed.dtype)
            g_query[i, :, lanes] = query_v[:half].astype(g_query.dtype)
            second = slice(width + lanes.start, width + lanes.stop)
            back[i, :, lanes] = mixed_v[half:].astype(back.dtype)
            back[i, :, second] = query_v[half:].astype(back.dtype)
            g_kv[i, :, lanes] = key_v.astype(g_kv.dtype)
            g_kv[i, :, second] = value_v.astype(g_kv.dtype)

        query_v = jnp.concatenate([query[i], guest[i, :, :width]], axis=0)
        grad_v = jnp.concatenate([grad[i], guest[i, :, width:]], axis=0)
        part_grads(query_v, *halves(kv, i), grad_v, mask, packed, load, store)

    columns, keys, _ = g_kv.shape
    flat = g_kv[...].reshape(columns * keys, 2 * width)
    for at in range(0, width, TILE):
        part = dot(flat[:, :width], key_weight[0, at : at + TILE, :], NT)
        part = part + dot(flat[:, width:], value_weight[0, at : at + TILE, :], NT)
        part = part.astype(g_kv.dtype).reshape(columns, keys, TILE)
        for b, term in enumerate(terms):
            term[:, :, at : at + TILE] = part[:, b * half : (b + 1) * half]


def call(kernel, steps, in_specs, out_specs, out_shapes, flops, operands):
    return pl.pallas_call(
        kernel,
        grid=(steps,),
        in_specs=in_specs,
        out_specs=out_specs,
        out_shape=out_shapes,
        compiler_params=pltpu.CompilerParams(vmem_limit_bytes=VMEM_LIMIT),
        cost_estimate=pl.CostEstimate(flops=flops, bytes_accessed=flops // 1000, transcendentals=0),
    )(*operands)


def block(shape, offset=0):
    rest = (0,) * (len(shape) - 1)
    return pl.BlockSpec(shape, lambda s: (s + offset,) + rest)


def whole(shape):
    return pl.BlockSpec(shape, lambda s: (0,) * len(shape))


SCALARS = pl.BlockSpec(memory_space=pltpu.SMEM)


def row_stats(scalars, qkv, grad):
    rows, count, width = grad.shape
    packed = max(1, min(HEADS, 256 // count))
    step = math.gcd(rows, ROW_STEP)
    return call(
        functools.partial(row_stats_kernel, packed),
        rows // step,
        [SCALARS, block((step, count, 3 * width)), block((step, count, width))],
        block((step, 3, HEADS * count)),
        jax.ShapeDtypeStruct((rows, 3, HEADS * count), jnp.float32),
        4 * rows * count * count * width * 4,
        (scalars, qkv, grad),
    )


def row_grads(scalars, stats, qkv, grad):
    rows, count, width = grad.shape
    packed = max(1, min(HEADS, 256 // count))
    step = math.gcd(rows, ROW_STEP)
    one, three = block((step, count, width)), block((step, count, 3 * width))
    return call(
        functools.partial(row_grads_kernel, packed),
        rows // step,
        [SCALARS, block((step, 3, HEADS * count)), three, one],
        [one, three],
        [jax.ShapeDtypeStruct(x.shape, jnp.bfloat16) for x in (grad, qkv)],
        12 * rows * count * count * width * 4,
        (scalars, stats, qkv, grad),
    )


def col_sizes(query):
    columns, half, width = query.shape
    packed = max(1, min(HEADS, 256 // (2 * half)))
    return half, packed, columns, math.gcd(columns, COL_STEP), width


def weights_of(weight):
    one = (1,) + weight.shape[1:]
    return [pl.BlockSpec(one, lambda s, j=j: (j, 0, 0)) for j in (1, 2)]


def col_stats(scalars, key_rows, query_rows, query, guest, grad, weight, held, stride):
    half, packed, columns, step, width = col_sizes(query)
    keys = half * len(held)
    own = block((step, half, width))
    stat = block((step, 3, HEADS * 2 * half))
    shape = jax.ShapeDtypeStruct((columns, 3, HEADS * 2 * half), jnp.float32)
    large = jax.ShapeDtypeStruct((columns, keys, 2 * width), jnp.bfloat16)
    joined = jax.ShapeDtypeStruct((columns, keys, width), jnp.bfloat16)
    return call(
        functools.partial(col_stats_kernel, packed, stride),
        columns // step,
        [SCALARS, whole(key_rows.shape), whole(query_rows.shape)]
        + [own, block((step, half, 2 * width)), own]
        + weights_of(weight)
        + [own] * len(held),
        [stat, stat, block((step, keys, 2 * width)), block((step, keys, width))],
        [shape, shape, large, joined],
        4 * columns * keys * width * (2 * half * 4 + width),
        (scalars, key_rows, query_rows, query, guest, grad, weight, weight, *held),
    )


def col_grads(
    scalars, key_rows, query_rows, row_part, own_part, other_part,
    query, guest, kv, grad, weight, offset, stride,
):
    half, packed, columns, step, width = col_sizes(query)
    keys = kv.shape[1]
    blocks = keys // half
    own = block((step, half, width))
    both = block((step, half, 2 * width))
    pair = block((step, keys, 2 * width))
    stat = block((step, 3, HEADS * 2 * half))
    stat_off = block((step, 3, HEADS * 2 * half), offset // step)
    shape = jax.ShapeDtypeStruct((columns, 3, HEADS * 2 * half), jnp.float32)
    small = jax.ShapeDtypeStruct((columns, half, width), jnp.bfloat16)
    twice = jax.ShapeDtypeStruct((columns, half, 2 * width), jnp.bfloat16)
    large = jax.ShapeDtypeStruct(kv.shape, jnp.bfloat16)
    return call(
        functools.partial(col_grads_kernel, packed, stride),
        columns // step,
        [SCALARS, whole(key_rows.shape), whole(query_rows.shape), stat_off, stat, stat]
        + [own, both, pair, own]
        + weights_of(weight),
        [stat, own, own, both, pair] + [own] * blocks,
        [shape, small, small, twice, large] + [small] * blocks,
        4 * columns * keys * width * (6 * half * 4 + width),
        (scalars, key_rows, query_rows, row_part, own_part, other_part)
        + (query, guest, kv, grad, weight, weight),
    )


def product(values, weight):
    return jnp.einsum("...d,df->...f", values, weight, preferred_element_type=jnp.float32)


def product_t(values, weight):
    return jnp.einsum("...f,df->...d", values, weight, preferred_element_type=jnp.float32)


def weight_product(values, grads):
    return jnp.einsum("abd,abf->df", values, grads, preferred_element_type=jnp.float32)


def narrow(values):
    return values.astype(jnp.bfloat16)


def body(tokens, lengths, w_qkv, out_grad):
    seq_count = lax.axis_size("seq")
    seq_index = lax.axis_index("seq")
    chips = seq_count // 2
    chip, core = seq_index // 2, seq_index % 2
    seq_local, row_local, columns, width = tokens.shape
    half_cols = columns // 2
    chip_rows = 2 * row_local
    group = half_cols // GROUPS
    w_q = w_qkv[0]
    w_all = jnp.concatenate([w_qkv[0], w_qkv[1], w_qkv[2]], axis=1)

    def pairs(links):
        return [(2 * a + c, 2 * b + c) for a, b in links for c in (0, 1)]

    swap = [(i, i ^ 1) for i in range(seq_count)]
    up = {k: pairs([(z - 1, z) for z in range(k, chips - 1)]) for k in range(1, chips - 1)}
    down = {k: [(b, a) for a, b in up[k]] for k in up}
    guest_up = pairs([(chips - 2, chips - 1)])
    guest_down = pairs([(chips - 1, chips - 2)])

    def send(values, perm):
        return lax.ppermute(values, "seq", perm)

    def to_columns(values, axis, row_axis):
        mine = lax.dynamic_slice_in_dim(values, core * half_cols, half_cols, axis)
        others = lax.dynamic_slice_in_dim(values, (1 - core) * half_cols, half_cols, axis)
        return jnp.concatenate([mine, send(others, swap)], axis=row_axis)

    def to_rows(values, axis, row_axis):
        mine = lax.slice_in_dim(values, 0, row_local, axis=row_axis)
        others = send(lax.slice_in_dim(values, row_local, chip_rows, axis=row_axis), swap)
        return jnp.where(
            core == 0,
            jnp.concatenate([mine, others], axis=axis),
            jnp.concatenate([others, mine], axis=axis),
        )

    tokens_r, grad_r = tokens[0], out_grad[0]
    limit = lengths[0]


    def by_group(values):
        values = jnp.swapaxes(values, 0, 1)
        mine = lax.dynamic_slice_in_dim(values, core * half_cols, half_cols, 0)
        others = lax.dynamic_slice_in_dim(values, (1 - core) * half_cols, half_cols, 0)
        items = []
        for g in range(GROUPS):
            part = slice(g * group, (g + 1) * group)
            items.append(jnp.concatenate([mine[part], send(others[part], swap)], axis=1))
        return items

    tokens_c, grad_c = by_group(tokens_r), by_group(grad_r)

    order = (jnp.arange(chip_rows, dtype=jnp.int32) + core * row_local) % chip_rows
    key_ids = []
    for k in range(chips - 2, -1, -1):
        valid = (chip >= k) & (chip <= chips - 2) if k > 0 else chip >= 0
        key_ids.append(jnp.where(valid, (chip - k) * chip_rows + order, FAR))
    key_ids = jnp.concatenate(key_ids)
    query_ids = jnp.concatenate(
        [chip * chip_rows + order, jnp.where(chip == chips - 2, (chip + 1) * chip_rows + order, -1)]
    )
    packed = max(1, min(HEADS, 256 // (2 * chip_rows)))
    lane = min(128, packed * 2 * chip_rows)
    key_rows = jnp.broadcast_to(key_ids[:, None], (key_ids.shape[0], lane))
    query_rows = jnp.broadcast_to(jnp.tile(query_ids, packed)[None], (8, packed * 2 * chip_rows))

    hops = chips - 2
    live = dict(tokens_c=tokens_c, grad_c=grad_c, tokens_r=tokens_r, grad_r=grad_r)
    live["held"] = [[tokens_c[g]] for g in range(GROUPS)]
    row_scalars = jnp.stack([limit, seq_index * row_local]).astype(jnp.int32)
    cross = guest_up + guest_down
    names = ("guest", "kv", "own", "other", "final", "mixed", "query", "terms")
    names += ("back", "moving", "swapped", "w_parts", "query_c")
    live.update({name: [None] * GROUPS for name in names})

    def scalars_of(g):
        return jnp.stack([limit, core * half_cols + g * group]).astype(jnp.int32)

    def step(g, s):
        if 0 <= s < hops:
            live["held"][g].append(send(live["held"][g][-1], up[s + 1]))
        if s == max(hops - 2, 0):
            live["query_c"][g] = narrow(product(live["tokens_c"][g], w_q))
        if s == hops - 1:
            visit = jnp.concatenate([live["query_c"][g], live["grad_c"][g]], axis=2)
            live["guest"][g] = send(visit, guest_down)
        if s == hops:
            live["own"][g], crossed, live["kv"][g], live["held"][g] = col_stats(
                scalars_of(g), key_rows, query_rows,
                live["query_c"][g], live["guest"][g], live["grad_c"][g],
                w_qkv, live["held"][g][::-1], columns
            )
            live["other"][g] = send(crossed, cross)
        if s == hops + 1:
            row_part = live["row_part"]
            if g + 1 < GROUPS:
                row_part, live["own"][g + 1] = lax.optimization_barrier((row_part, live["own"][g + 1]))
            final, mixed, g_query, back, g_kv, *terms = col_grads(
                scalars_of(g), key_rows, query_rows, row_part, live["own"][g], live["other"][g],
                live["query_c"][g], live["guest"][g], live["kv"][g], live["grad_c"][g],
                w_qkv, g * group, columns
            )
            live["final"][g], live["mixed"][g], live["query"][g] = final, mixed, g_query
            live["kv"][g], live["back"][g], live["terms"][g] = g_kv, back, terms
        if s == hops + 2:
            back = live["back"][g]
            live["back"][g] = send(back, guest_up)
        if s == hops + 3:
            back = live["back"][g]
            live["mixed"][g] = narrow(
                live["mixed"][g].astype(jnp.float32) + back[..., :width].astype(jnp.float32)
            )
            live["query"][g] = narrow(
                live["query"][g].astype(jnp.float32) + back[..., width:].astype(jnp.float32)
            )
            live["swapped"][g] = send(live["mixed"][g][:, row_local:], swap)
            live["w_parts"][g] = [
                narrow(weight_product(live["tokens_c"][g], live["query"][g])),
                narrow(weight_product(live["held"][g], live["kv"][g])),
            ]
        if hops + 2 <= s <= 2 * hops + 2:
            k = 2 * hops + 2 - s
            term = live["terms"][g][hops - k]
            if k < hops:
                term = term.astype(jnp.float32) + live["moving"][g].astype(jnp.float32)
            if k > 0:
                live["moving"][g] = send(narrow(term), down[k])
            else:
                own = narrow(term + product_t(live["query"][g], w_q))
                live["moving"][g] = (own[:, :row_local], send(own[:, row_local:], swap))

    for t in range(GROUPS + 2 * hops + 2):
        if t == 0:
            live["rows"] = narrow(product(live["tokens_r"], w_all))
        if t == 1:
            part = row_stats(row_scalars, live["rows"], live["grad_r"])
            part = part.reshape(row_local, 3, HEADS, columns).transpose(3, 1, 2, 0)
            part = to_columns(part, 0, 3)
            part = jnp.concatenate([part, send(part, guest_down)], axis=3)
            live["row_part"] = part.reshape(half_cols, 3, HEADS * 2 * chip_rows)
        if t == GROUPS + hops + 1:
            final = jnp.concatenate(live["final"], axis=0).reshape(half_cols, 3, HEADS, 2 * chip_rows)
            final = to_rows(final[..., :chip_rows], 0, 3)
            final = final.transpose(3, 1, 2, 0).reshape(row_local, 3, HEADS * columns)
            live["row_grads"] = row_grads(row_scalars, final, live["rows"], live["grad_r"])
        if t == GROUPS + hops + 2:
            live["w_row"] = weight_product(live["tokens_r"], live["row_grads"][1])
        for g in sorted(range(GROUPS), key=lambda g: t - g != hops):
            step(g, t - g)
        live = lax.optimization_barrier(live)

    def assemble(mine, others):
        mine, others = jnp.concatenate(mine, axis=0), jnp.concatenate(others, axis=0)
        joined = jnp.where(
            core == 0,
            jnp.concatenate([mine, others], axis=0),
            jnp.concatenate([others, mine], axis=0),
        )
        return jnp.swapaxes(joined, 0, 1).astype(jnp.float32)

    mixed_r, row_g = live["row_grads"]
    mixed_b = assemble([item[:, :row_local] for item in live["mixed"]], live["swapped"])
    attention = narrow(mixed_r.astype(jnp.float32) + mixed_b)
    terms_b = assemble(*zip(*live["moving"]))
    input_grad = narrow(product_t(row_g, w_all) + terms_b)

    shares = []
    for j in range(3):
        place = slice(j * width, (j + 1) * width)
        total = live["w_row"][:, place]
        for first, second in live["w_parts"]:
            part = first if j == 0 else second[:, (j - 1) * width : j * width]
            total = total + part.astype(jnp.float32)
        total = narrow(total).reshape(chips, 2, width // seq_count, width)
        mine = lax.dynamic_index_in_dim(total, core, 1, keepdims=False)
        others = lax.dynamic_index_in_dim(total, 1 - core, 1, keepdims=False)
        shares.append(narrow(mine.astype(jnp.float32) + send(others, swap).astype(jnp.float32)))
    share = jnp.stack(shares)
    share = lax.psum_scatter(share, "dp", scatter_dimension=3, tiled=True)
    rings = [[2 * z + c for z in range(chips)] for c in (0, 1)]
    share = lax.psum_scatter(share, "seq", scatter_dimension=1, axis_index_groups=rings, tiled=True)
    w_grads = share[:, 0].astype(jnp.float32)
    return (attention[None], input_grad[None], w_grads)


def solution(mesh):
    in_specs = (P("dp", "seq", None, None), P("dp"), P(), P("dp", "seq", None, None))
    out_specs = (P("dp", "seq", None, None), P("dp", "seq", None, None), P(None, "seq", "dp"))
    return jax.shard_map(body, mesh=mesh, in_specs=in_specs, out_specs=out_specs, check_vma=False)
```
